32 devices in a mesh: ctx: 8 (over z, y), head: 4 (over x, core).
Axes of the slice: x: 2, y: 2, z: 4, core: 2. Of those that a mesh axis runs over, the one named last changes fastest.
Arguments:
- queries: bfloat16 [8192, 512], P(('ctx', 'head')), may hold values from -27 to 27
- token_keys: bfloat16 [8192, 512], P(('ctx', 'head')), may hold values from -6 to 6
- token_values: bfloat16 [8192, 512], P(('ctx', 'head')), may hold values from -6 to 6
- grad_out: bfloat16 [8192, 512], P(('ctx', 'head')), may hold values from -48 to 48
- clip_gate: bfloat16 [16, 512], P(None, 'head'), may hold values from 0.099609375 to 1.8984375
- clip_lengths: int32 [16], replicated, may hold values from 1 to 1024, 8192 in all
Outputs:
- grad_queries: bfloat16 [8192, 512], P(('ctx', 'head'))
- grad_keys: bfloat16 [8192, 512], P(('ctx', 'head'))
- grad_values: bfloat16 [8192, 512], P(('ctx', 'head'))
- grad_gate: float32 [16, 512], P(None, 'head')
The draws below stay inside these ranges and needn't reach their ends.
Inputs may be any that keep to these rules, and one draw needn't show every extreme that they name: `clip_lengths`: the clips fill the window in order; each attends only within itself.
All inputs are finite; a program needn't handle non-finite values.
Results may differ from the reference program's by a relative error of at most 0.03.
Values may be sent and summed in bfloat16 or wider, within the bound.
No kernel may reach another device: no remote copies, remote signals or barrier semaphores. Data moves between devices by JAX's collectives and lax.ppermute only.
A program may use at most 64 MiB of HBM per device.

```python
import math
import jax
import jax.numpy as jnp
import numpy as np
from jax import lax

DH = 128
TOK_DEV = 1024
REACH = 1
HEADS = 4
TOKENS = 8192
NCLIP = 16
CLIP_MOST = 1024


def drawn_pair(key):
    full_shape = (TOKENS, HEADS * DH)
    base_keys = jnp.clip(jax.random.normal(jax.random.fold_in(key, 11), full_shape, jnp.float32), -6.0, 6.0)
    base_queries = jnp.clip(jax.random.normal(jax.random.fold_in(key, 12), full_shape, jnp.float32), -6.0, 6.0)
    return (base_queries, base_keys)


def draw_queries(key, part):
    return drawn_pair(key)[0].astype(jnp.bfloat16)


def draw_token_keys(key, part):
    return drawn_pair(key)[1].astype(jnp.bfloat16)


def steps_of(own_key, shape, shards, low, top_value):
    loudness = 1.0
    for position, blocks in shards:
        heights = jax.random.uniform(jax.random.fold_in(jax.random.fold_in(own_key, 6), position), (blocks,), jnp.float32, low / len(shards), top_value / len(shards))
        loudness = loudness * jnp.repeat(jnp.exp(heights), shape[position] // blocks).reshape((-1,) + (1,) * (len(shape) - 1 - position))
    return loudness


def split_up(amount, total, bound, lean):
    weights = [(1 << 20) // math.isqrt(grade ** lean) + 1 for grade in range(2, amount + 1)]
    spare, holding = total - bound - (amount - 1), [1] * (amount - 1)
    while spare > 0:
        candidates = [i for i in range(amount - 1) if holding[i] < bound]
        mass, remaining = sum([weights[i] for i in candidates]), spare
        for i in candidates:
            more = min(bound - holding[i], max(1, remaining * weights[i] // mass), spare)
            holding[i] = holding[i] + more
            spare = spare - more
    return np.array([bound] + holding)


def uneven_parts(rng, number_of, total, most, slope):
    if number_of == 2:
        one = jax.random.randint(rng, (), max(1, total - most), min(most, total - 1) + 1)
        return jnp.stack([one, total - one])
    lengths = jnp.asarray(split_up(number_of, total, most, slope), jnp.int32)
    pairs = (number_of - 1) // 2
    source_of, sink = lengths[1:1 + 2 * pairs:2], lengths[2:2 + 2 * pairs:2]
    slack = jnp.minimum(source_of - 1, most - sink)
    moved = jax.random.randint(jax.random.fold_in(rng, 1), (pairs,), 0, 1 << 20) % (slack + 1)
    lengths = lengths.at[1:1 + 2 * pairs:2].set(source_of - moved).at[2:2 + 2 * pairs:2].set(sink + moved)
    return lengths[jax.random.permutation(jax.random.fold_in(rng, 2), number_of)]


def centred(own_key, dims, width, most, split=(), held_as=jnp.bfloat16):
    values = jax.random.normal(own_key, dims, jnp.float32) * width
    if len(split) > 0:
        values = steps_of(own_key, dims, split, -0.22, 0.18) * values
    return jnp.clip(values, min=-most, max=most).astype(held_as)


def setup_inputs(seed: int = 0) -> dict:
    splits = jax.random.split(jax.random.key(seed), 7)
    queries = draw_queries(jax.random.fold_in(splits[6], 71), 0)
    token_keys = draw_token_keys(jax.random.fold_in(splits[6], 71), 0)
    token_values = centred(splits[2], (TOKENS, HEADS * DH), 1.0, 6.0, ((0, 32),))
    grad_out = centred(splits[3], (TOKENS, HEADS * DH), 8.0, 48.0, ((0, 32),))
    clip_gate = jnp.clip(1.0 + 0.18 * jax.random.normal(splits[4], (NCLIP, HEADS * DH), jnp.float32), 0.099609375, 1.8984375).astype(jnp.bfloat16)
    clip_lengths = uneven_parts(splits[5], NCLIP, TOKENS, CLIP_MOST, 2).astype(jnp.int32)
    return {"queries": queries, "token_keys": token_keys, "token_values": token_values, "grad_out": grad_out, "clip_gate": clip_gate, "clip_lengths": clip_lengths}


def clip_of(positions, clip_ends):
    return jnp.sum((positions[:, None] >= clip_ends[None, :]).astype(jnp.int32), axis=1).astype(jnp.int32)


def split_pair(numbers):
    upper_part = numbers.astype(jnp.bfloat16)
    lower_part = (numbers - upper_part.astype(jnp.float32)).astype(jnp.bfloat16)
    return upper_part.astype(jnp.float32) + lower_part.astype(jnp.float32)


def reference(queries, token_keys, token_values, grad_out, clip_gate, clip_lengths):
    scaling = DH ** -0.5
    clip_ends = jnp.cumsum(clip_lengths).astype(jnp.int32)
    positions = jnp.arange(TOKENS, dtype=jnp.int32)
    token_clip = clip_of(positions, clip_ends)
    onehot = (token_clip[:, None] == jnp.arange(NCLIP, dtype=jnp.int32)[None, :]).astype(jnp.float32)
    gate_rows = clip_gate.astype(jnp.float32)[token_clip]
    d_out_all = (gate_rows * grad_out.astype(jnp.float32)).astype(jnp.bfloat16)
    block_rows = TOK_DEV
    block_count = TOKENS // TOK_DEV
    pad_rows = REACH * TOK_DEV
    window = (2 * REACH + 1) * TOK_DEV
    filler = jnp.full((pad_rows,), -1, jnp.int32)
    clip_padded = jnp.concatenate([filler, token_clip, filler]).astype(jnp.int32)
    grads_q, grads_k, grads_v, grads_gate = [], [], [], []
    for head_index in range(HEADS):
        low_col = head_index * DH
        my_query = queries[:, low_col:low_col + DH]
        my_keys = token_keys[:, low_col:low_col + DH]
        my_values = token_values[:, low_col:low_col + DH]
        my_dout = d_out_all[:, low_col:low_col + DH]
        my_grad = grad_out[:, low_col:low_col + DH]
        keys_padded = jnp.pad(my_keys, ((pad_rows, pad_rows), (0, 0)))
        values_padded = jnp.pad(my_values, ((pad_rows, pad_rows), (0, 0)))

        def forward_block(block_index):
            first_row = (block_index * block_rows).astype(jnp.int32)
            query_block = lax.dynamic_slice_in_dim(my_query, first_row, block_rows, 0)
            dout_block = lax.dynamic_slice_in_dim(my_dout, first_row, block_rows, 0)
            clip_block = lax.dynamic_slice_in_dim(token_clip, first_row, block_rows, 0)
            key_window = lax.dynamic_slice_in_dim(keys_padded, first_row, window, 0)
            value_window = lax.dynamic_slice_in_dim(values_padded, first_row, window, 0)
            clip_window = lax.dynamic_slice_in_dim(clip_padded, first_row, window, 0)
            same_clip = clip_block[:, None] == clip_window[None, :]
            scores = jnp.dot(query_block, key_window.T, preferred_element_type=jnp.float32) * scaling
            scores = jnp.where(same_clip, scores, -jnp.inf)
            row_max = jnp.max(scores, axis=1)
            log_total = row_max + jnp.log(jnp.sum(jnp.exp(scores - row_max[:, None]), axis=1))
            probs = jnp.exp(scores - log_total[:, None])
            probs_low = probs.astype(jnp.bfloat16)
            grad_probs = jnp.dot(dout_block, value_window.T, preferred_element_type=jnp.float32)
            weighted = (probs * grad_probs).astype(jnp.bfloat16)
            output = jnp.dot(probs_low, value_window, preferred_element_type=jnp.float32)
            row_dot = jnp.sum(dout_block.astype(jnp.float32) * output, axis=1)
            grad_query = scaling * (jnp.dot(weighted, key_window, preferred_element_type=jnp.float32)
                                    - row_dot[:, None] * jnp.dot(probs_low, key_window, preferred_element_type=jnp.float32))
            return log_total, row_dot, output, grad_query

        log_total, row_dot, output, grad_query = lax.map(forward_block, jnp.arange(block_count, dtype=jnp.int32))
        log_total = log_total.reshape(TOKENS)
        row_dot = row_dot.reshape(TOKENS)
        output = output.reshape(TOKENS, DH)
        grad_query = grad_query.reshape(TOKENS, DH)
        gate_term = jnp.dot(onehot.T, my_grad.astype(jnp.float32) * output, precision=lax.Precision.HIGHEST)
        log_pair = split_pair(log_total)
        dot_pair = split_pair(row_dot)

        def backward_block(carried, block_index):
            acc_keys, acc_values = carried
            first_row = (block_index * block_rows).astype(jnp.int32)
            query_block = lax.dynamic_slice_in_dim(my_query, first_row, block_rows, 0)
            dout_block = lax.dynamic_slice_in_dim(my_dout, first_row, block_rows, 0)
            clip_block = lax.dynamic_slice_in_dim(token_clip, first_row, block_rows, 0)
            log_block = lax.dynamic_slice_in_dim(log_pair, first_row, block_rows, 0)
            dot_block = lax.dynamic_slice_in_dim(dot_pair, first_row, block_rows, 0)
            key_window = lax.dynamic_slice_in_dim(keys_padded, first_row, window, 0)
            value_window = lax.dynamic_slice_in_dim(values_padded, first_row, window, 0)
            clip_window = lax.dynamic_slice_in_dim(clip_padded, first_row, window, 0)
            same_clip = clip_block[:, None] == clip_window[None, :]
            scores = jnp.dot(query_block, key_window.T, preferred_element_type=jnp.float32) * scaling
            probs = jnp.exp(jnp.where(same_clip, scores - log_block[:, None], -jnp.inf))
            grad_probs = jnp.dot(dout_block, value_window.T, preferred_element_type=jnp.float32)
            grad_scores = (probs * (grad_probs - dot_block[:, None])).astype(jnp.bfloat16)
            value_term = jnp.dot(probs.astype(jnp.bfloat16).T, dout_block, preferred_element_type=jnp.float32)
            key_term = jnp.dot(grad_scores.T, query_block, preferred_element_type=jnp.float32)
            acc_values = lax.dynamic_update_slice_in_dim(
                acc_values, lax.dynamic_slice_in_dim(acc_values, first_row, window, 0) + value_term, first_row, 0)
            acc_keys = lax.dynamic_update_slice_in_dim(
                acc_keys, lax.dynamic_slice_in_dim(acc_keys, first_row, window, 0) + key_term, first_row, 0)
            return (acc_keys, acc_values), None

        zero_grads = jnp.zeros((TOKENS + 2 * pad_rows, DH), jnp.float32)
        (acc_keys, acc_values), _ = lax.scan(backward_block, (zero_grads, zero_grads), jnp.arange(block_count, dtype=jnp.int32))
        acc_keys = acc_keys[pad_rows:pad_rows + TOKENS]
        acc_values = acc_values[pad_rows:pad_rows + TOKENS]
        grads_q.append(grad_query.astype(jnp.bfloat16))
        grads_k.append((scaling * acc_keys).astype(jnp.bfloat16))
        grads_v.append(acc_values.astype(jnp.bfloat16))
        grads_gate.append(gate_term)
    return (jnp.concatenate(grads_q, axis=1), jnp.concatenate(grads_k, axis=1),
            jnp.concatenate(grads_v, axis=1), jnp.concatenate(grads_gate, axis=1))
```

```python
import functools
import math

import jax
import jax.numpy as jnp
from jax import lax
from jax.experimental import pallas as pl
from jax.experimental.pallas import tpu as pltpu
from jax.sharding import PartitionSpec as P

AXES = ("ctx", "head")
TILE = 256
NEG = -1e30
NT = (((1,), (1,)), ((), ()))
NN = (((1,), (0,)), ((), ()))


def dot(left, right, dims):
    return lax.dot_general(left, right, dims, preferred_element_type=jnp.float32)


def toward(shift, blocks, heads):
    pairs = []
    for i in range(blocks):
        for j in range(heads):
            target = i + 1 if j >= heads // 2 else i - 1
            if 0 <= target < blocks:
                pairs.append((i * heads + j, target * heads + (j + shift) % heads))
    return pairs


def back(shift, blocks, heads):
    return [(b, a) for a, b in toward(shift, blocks, heads)]


def attention_kernel(geometry, meta, own, *refs):
    heads, rows, pad, width, scaling = geometry
    part = rows // heads
    halos, refs = refs[:heads], refs[heads:]
    gate, key_id, query_id, own_out = refs[:4]
    halo_outs, refs = refs[4 : 4 + heads], refs[4 + heads :]
    gate_out, win, result, d_out, gates, keys_t, score, dprob, acc_k, acc_v, sem = refs
    window = rows + 2 * pad
    tiles = window // TILE
    per_exp = scaling * math.log2(math.e)
    me = meta[2 * tiles]
    clips = gate.shape[0]

    places = [(j, pad + rows + j * part if j < heads // 2 else (j - heads // 2) * part) for j in range(heads)]

    first = pltpu.make_async_copy(own, win.at[pl.ds(pad, rows), :], sem.at[0])
    first.start()
    for j, place in places:
        slot = lax.rem(me + heads - j, heads)
        for r in range(heads):
            @pl.when(slot == r)
            def _():
                pltpu.make_async_copy(halos[r], win.at[pl.ds(place, part), :], sem.at[1 + j]).start()
    first.wait()
    for j, place in places:
        pltpu.make_async_copy(halos[0], win.at[pl.ds(place, part), :], sem.at[1 + j]).wait()

    def prepare(t, _):
        at = pl.ds(pl.multiple_of(t * TILE, TILE), TILE)
        lanes = lax.broadcasted_iota(jnp.int32, (TILE, clips), 1)
        onehot = (key_id[at, :] == lanes).astype(jnp.float32).astype(jnp.bfloat16)
        row_gates = dot(onehot, gate[...], NN)
        gates[at, :] = row_gates
        d_out[at, :] = (row_gates * win[at, 3 * width :].astype(jnp.float32)).astype(jnp.bfloat16)
        keys_t[:, at] = win[at, width : 2 * width].T
        acc_k[at, :] = jnp.zeros((TILE, width), jnp.float32)
        acc_v[at, :] = jnp.zeros((TILE, width), jnp.float32)
        return 0

    lax.fori_loop(0, tiles, prepare, 0)

    def query_tile(t, _):
        low, high = meta[t], meta[tiles + t]

        @pl.when(high > low)
        def _():
            q_at = pl.ds(pl.multiple_of(t * TILE, TILE), TILE)
            query = win[q_at, :width]
            cotangent = d_out[q_at, :]
            ids = query_id[:, q_at]

            def scores(k, top):
                at = pl.ds(pl.multiple_of(k * TILE, TILE), TILE)
                s = dot(win[at, width : 2 * width], query, NT)
                s = jnp.where(key_id[at, :] == ids, s, NEG)
                score[at, :] = s
                return jnp.maximum(top, jnp.max(s.reshape(TILE // 8, 8, TILE), axis=0))

            top = lax.fori_loop(low, high, scores, jnp.full((8, TILE), NEG, jnp.float32))
            top = jnp.max(top, axis=0, keepdims=True) * per_exp

            def weigh(k, carried):
                total, weighted = carried
                at = pl.ds(pl.multiple_of(k * TILE, TILE), TILE)
                p = jnp.exp2(score[at, :] * per_exp - top)
                dp = dot(win[at, 2 * width : 3 * width], cotangent, NT)
                score[at, :] = p
                dprob[at, :] = dp
                return (
                    total + jnp.sum(p.reshape(TILE // 8, 8, TILE), axis=0),
                    weighted + jnp.sum((p * dp).reshape(TILE // 8, 8, TILE), axis=0),
                )

            zero = jnp.zeros((8, TILE), jnp.float32)
            total, weighted = lax.fori_loop(low, high, weigh, (zero, zero))
            total = jnp.sum(total, axis=0, keepdims=True)
            inverse = jnp.where(ids >= 0, 1.0 / total, 0.0)
            row_dot = jnp.sum(weighted, axis=0, keepdims=True) * inverse
            grad = win[q_at, 3 * width :]

            def gradients(k, acc_q):
                at = pl.ds(pl.multiple_of(k * TILE, TILE), TILE)
                p = score[at, :] * inverse
                g = (p * (dprob[at, :] - row_dot)).astype(jnp.bfloat16)
                acc_v[at, :] += dot(p.astype(jnp.bfloat16), grad, NN)
                acc_k[at, :] += dot(g, query, NN)
                return acc_q + dot(keys_t[:, at], g, NN)

            acc_q = lax.fori_loop(low, high, gradients, jnp.zeros((width, TILE), jnp.float32))
            result[q_at, :width] = (acc_q * scaling).T.astype(jnp.bfloat16)

        return 0

    lax.fori_loop(0, tiles, query_tile, 0)

    gate_out[...] = jnp.zeros_like(gate_out)

    def finish(t, _):
        @pl.when(meta[tiles + t] > meta[t])
        def _():
            at = pl.ds(pl.multiple_of(t * TILE, TILE), TILE)
            summed = acc_v[at, :]
            result[at, width : 2 * width] = (acc_k[at, :] * scaling).astype(jnp.bfloat16)
            result[at, 2 * width :] = (summed * gates[at, :]).astype(jnp.bfloat16)
            term = summed * win[at, 2 * width : 3 * width].astype(jnp.float32)
            lanes = lax.broadcasted_iota(jnp.int32, (TILE, clips), 1)
            onehot = (key_id[at, :] == lanes).astype(jnp.float32)
            gate_out[...] += lax.dot_general(
                onehot,
                term,
                (((0,), (0,)), ((), ())),
                precision=lax.Precision.HIGHEST,
                preferred_element_type=jnp.float32,
            )

        return 0

    lax.fori_loop(0, tiles, finish, 0)

    last = pltpu.make_async_copy(result.at[pl.ds(pad, rows), :], own_out, sem.at[0])
    last.start()
    for j, place in places:
        slot = lax.rem(me + heads - j, heads)
        for r in range(heads):
            @pl.when(slot == r)
            def _():
                pltpu.make_async_copy(result.at[pl.ds(place, part), :], halo_outs[r], sem.at[1 + j]).start()
    last.wait()
    for j, place in places:
        pltpu.make_async_copy(result.at[pl.ds(place, part), :], halo_outs[0], sem.at[1 + j]).wait()


def attention(meta, own, halos, gate, key_id, query_id, heads, pad, width):
    rows = own.shape[0]
    part = rows // heads
    window = rows + 2 * pad
    anywhere = pl.BlockSpec(memory_space=pl.ANY)
    vmem = pl.BlockSpec(memory_space=pltpu.VMEM)
    geometry = (heads, rows, pad, width, width ** (-0.5))
    f32, b16 = jnp.float32, jnp.bfloat16
    return pl.pallas_call(
        functools.partial(attention_kernel, geometry),
        out_shape=[jax.ShapeDtypeStruct((rows, 3 * width), b16)]
        + [jax.ShapeDtypeStruct((part, 3 * width), b16)] * heads
        + [jax.ShapeDtypeStruct(gate.shape, f32)],
        in_specs=[pl.BlockSpec(memory_space=pltpu.SMEM)] + [anywhere] * (1 + heads) + [vmem] * 3,
        out_specs=[anywhere] * (1 + heads) + [vmem],
        scratch_shapes=[
            pltpu.VMEM((window, 4 * width), b16),
            pltpu.VMEM((window, 3 * width), b16),
            pltpu.VMEM((window, width), b16),
            pltpu.VMEM((window, width), f32),
            pltpu.VMEM((width, window), b16),
            pltpu.VMEM((window, TILE), f32),
            pltpu.VMEM((window, TILE), f32),
            pltpu.VMEM((window, width), f32),
            pltpu.VMEM((window, width), f32),
            pltpu.SemaphoreType.DMA((1 + heads,)),
        ],
        compiler_params=pltpu.CompilerParams(vmem_limit_bytes=48 * 1024 * 1024),
        cost_estimate=pl.CostEstimate(flops=4_000_000_000, bytes_accessed=4_000_000, transcendentals=4_000_000),
    )(meta, own, *halos, gate, key_id, query_id)


def choose_kernel(heads, width, mine, own, *refs):
    halos, outs = refs[:heads], refs[heads:]
    me = lax.axis_index("head")
    keep = mine[...] > 0
    for r in range(heads):
        head = lax.rem(me + r, heads)
        at = pl.ds(pl.multiple_of(head * width, width), width)
        kept, other = own[head], halos[r][...]
        for n, out in enumerate(outs):
            cols = slice(n * width, (n + 1) * width)
            out[:, at] = jnp.where(keep, kept[:, cols], other[:, cols])


def choose(mine, own, halos, heads, width):
    part = own.shape[1]
    return pl.pallas_call(
        functools.partial(choose_kernel, heads, width),
        out_shape=[jax.ShapeDtypeStruct((part, heads * width), jnp.bfloat16)] * 3,
        compiler_params=pltpu.CompilerParams(vmem_limit_bytes=32 * 1024 * 1024),
    )(mine, own, *halos)


def shards(heads, queries, token_keys, token_values, grad_out, clip_gate, clip_lengths):
    part, total_width = queries.shape
    width = total_width // heads
    rows = part * heads
    pad = rows // 2
    window = rows + 2 * pad
    tiles = window // TILE
    blocks = lax.axis_size("ctx")
    block, me = lax.axis_index("ctx"), lax.axis_index("head")

    packed = jnp.stack(
        [a.reshape(part, heads, width) for a in (queries, token_keys, token_values, grad_out)], axis=2
    ).transpose(1, 0, 2, 3).reshape(heads, part, 4 * width)
    own = lax.all_to_all(packed, "head", 0, 0, tiled=True).reshape(rows, 4 * width)
    halos = [
        lax.ppermute(
            lax.dynamic_index_in_dim(packed, lax.rem(me + r, heads), 0, keepdims=False),
            AXES,
            toward(r, blocks, heads),
        )
        for r in range(heads)
    ]

    ends = jnp.cumsum(clip_lengths)
    starts = ends - clip_lengths
    first_block, last_block = starts // rows, (ends - 1) // rows
    edge = last_block * rows
    owner = jnp.where((first_block == last_block) | (edge - starts < ends - edge), last_block, first_block)
    base = block * rows - pad
    owned = owner == block
    most = jnp.int32(2**30)
    low = jnp.min(jnp.where(owned, starts, most))
    high = jnp.max(jnp.where(owned, ends, 0))
    tile_low = base + TILE * jnp.arange(tiles, dtype=jnp.int32)
    first = jnp.maximum(tile_low, low)
    last = jnp.minimum(tile_low + TILE, high) - 1
    clip_low = jnp.max(jnp.where(starts[None, :] <= first[:, None], starts[None, :], 0), axis=1)
    clip_high = jnp.min(jnp.where(ends[None, :] > last[:, None], ends[None, :], most), axis=1)
    some = first <= last
    k_low = jnp.where(some, (clip_low - base) // TILE, 0)
    k_high = jnp.where(some, (clip_high - base + TILE - 1) // TILE, 0)
    meta = jnp.concatenate([k_low, k_high, me[None]]).astype(jnp.int32)

    def clip_ids(positions):
        ids = jnp.sum((positions[:, None] >= ends[None, :]).astype(jnp.int32), axis=1)
        return jnp.where((positions >= low) & (positions < high), ids, -1)

    ids = clip_ids(base + jnp.arange(window, dtype=jnp.int32))
    own_out, *rest = attention(
        meta, own, halos, clip_gate, ids[:, None], ids[None, :], heads, pad, width
    )
    halo_outs, gate_term = rest[:heads], rest[heads]

    homes = [lax.ppermute(halo_outs[r], AXES, back(r, blocks, heads)) for r in range(heads)]
    mixed = lax.all_to_all(own_out.reshape(heads, part, 3 * width), "head", 0, 0, tiled=True)

    step = 1
    while step < blocks:
        gate_term = gate_term + lax.ppermute(gate_term, "ctx", [(i, i ^ step) for i in range(blocks)])
        step *= 2

    mine = rows * block + part * me + jnp.arange(part, dtype=jnp.int32)
    mine = ((mine >= low) & (mine < high)).astype(jnp.int32)[:, None]
    grad_queries, grad_keys, grad_values = choose(mine, mixed, homes, heads, width)
    return grad_queries, grad_keys, grad_values, gate_term


def solution(mesh):
    rows, columns = P(AXES, None), P(None, "head")
    return jax.shard_map(
        functools.partial(shards, mesh.shape["head"]),
        mesh=mesh,
        in_specs=(rows, rows, rows, rows, columns, P()),
        out_specs=(rows, rows, rows, columns),
        check_vma=False,
    )
```

```python
import functools
import math

import jax
import jax.numpy as jnp
from jax import lax
from jax.experimental import pallas as pl
from jax.experimental.pallas import tpu as pltpu
from jax.sharding import PartitionSpec as P

AXES = ("ctx", "head")
NEG = -1e30
NT = (((1,), (1,)), ((), ()))
NN = (((1,), (0,)), ((), ()))


def dot(left, right, dims):
    return lax.dot_general(left, right, dims, preferred_element_type=jnp.float32)


def toward(shift, blocks, heads):
    pairs = []
    for i in range(blocks):
        for j in range(heads):
            target = i + 1 if j >= heads // 2 else i - 1
            if 0 <= target < blocks:
                pairs.append((i * heads + j, target * heads + (j + shift) % heads))
    return pairs


def back(shift, blocks, heads):
    return [(b, a) for a, b in toward(shift, blocks, heads)]


def pack_kernel(heads, width, *refs):
    arrays, packed, sends = refs[:4], refs[4], refs[5 : 5 + heads]
    held, sem = refs[5 + heads :]
    me = lax.axis_index("head")
    copies = [pltpu.make_async_copy(array, held.at[n], sem.at[n]) for n, array in enumerate(arrays)]
    for copy in copies:
        copy.start()
    for n, copy in enumerate(copies):
        copy.wait()
        cols = slice(n * width, (n + 1) * width)
        for h in range(heads):
            packed[h, :, cols] = held[n, :, h * width : (h + 1) * width]
        for r in range(heads):
            head = lax.rem(me + r, heads)
            sends[r][:, cols] = held[n, :, pl.ds(pl.multiple_of(head * width, width), width)]


def pack(arrays, heads, width):
    part = arrays[0].shape[0]
    one = jax.ShapeDtypeStruct((part, 4 * width), jnp.bfloat16)
    vmem = pl.BlockSpec(memory_space=pltpu.VMEM)
    return pl.pallas_call(
        functools.partial(pack_kernel, heads, width),
        out_shape=[jax.ShapeDtypeStruct((heads, part, 4 * width), jnp.bfloat16)] + [one] * heads,
        in_specs=[pl.BlockSpec(memory_space=pltpu.HBM)] * 4,
        out_specs=[vmem] * (1 + heads),
        scratch_shapes=[pltpu.VMEM((4, part, heads * width), jnp.bfloat16), pltpu.SemaphoreType.DMA((4,))],
        compiler_params=pltpu.CompilerParams(vmem_limit_bytes=60 * 1024 * 1024),
    )(*arrays)


def attention_kernel(geometry, place, lengths, own, *refs):
    heads, rows, pad, width, scaling = geometry
    part = rows // heads
    halos, refs = refs[:heads], refs[heads:]
    gate, own_out = refs[:2]
    halo_outs, refs = refs[2 : 2 + heads], refs[2 + heads :]
    gate_out, span_out, win, result, keys_t, acc_k, acc_v, starts, sem = refs
    window = rows + 2 * pad
    per_exp = scaling * math.log2(math.e)
    block, me = place[0], place[1]
    clips = gate.shape[0]

    places = [(j, pad + rows + j * part if j < heads // 2 else (j - heads // 2) * part) for j in range(heads)]

    first = pltpu.make_async_copy(own, win.at[pl.ds(pad, rows), :], sem.at[0])
    first.start()
    for j, at_row in places:
        slot = lax.rem(me + heads - j, heads)
        for r in range(heads):

            @pl.when(slot == r)
            def _():
                pltpu.make_async_copy(halos[r], win.at[pl.ds(at_row, part), :], sem.at[1 + j]).start()

    def place_clip(c, carried):
        start, clip_low, clip_high, low, high = carried
        end = start + lengths[c]
        first_block, last_block = lax.div(start, rows), lax.div(end - 1, rows)
        edge = last_block * rows
        lower = (first_block != last_block) & (edge - start >= end - edge)
        owned = jnp.where(lower, first_block, last_block) == block
        starts[c] = start
        return (
            end,
            jnp.where(owned, jnp.minimum(clip_low, c), clip_low),
            jnp.where(owned, c + 1, clip_high),
            jnp.where(owned, jnp.minimum(low, start), low),
            jnp.where(owned, end, high),
        )

    most, zero = jnp.int32(2**30), jnp.int32(0)
    _, clip_low, clip_high, low, high = lax.fori_loop(0, clips, place_clip, (zero, most, zero, most, zero))
    span_out[0] = low
    span_out[1] = high
    gate_out[...] = jnp.zeros_like(gate_out)
    win[window:, :] = jnp.zeros((win.shape[0] - window, 4 * width), jnp.bfloat16)

    first.wait()
    for j, at_row in places:
        pltpu.make_async_copy(halos[0], win.at[pl.ds(at_row, part), :], sem.at[1 + j]).wait()

    def whole_clip(key_rows, query_rows, c, base, head, tail):
        at = pl.ds(base, key_rows)
        keys_t[:, :key_rows] = win[at, width : 2 * width].T
        acc_k[:key_rows, :] = jnp.zeros((key_rows, width), jnp.float32)
        acc_v[:key_rows, :] = jnp.zeros((key_rows, width), jnp.float32)
        row_gate = gate[pl.ds(c, 1), :]
        key_row = lax.broadcasted_iota(jnp.int32, (key_rows, query_rows), 0)

        def query_tile(j, _):
            q_at = pl.ds(pl.multiple_of(base + j * query_rows, 16), query_rows)
            query, grad = win[q_at, :width], win[q_at, 3 * width :]
            d_out = (row_gate * grad.astype(jnp.float32)).astype(jnp.bfloat16)
            s = dot(win[at, width : 2 * width], query, NT)
            s = jnp.where((key_row >= head) & (key_row < tail), s, NEG)
            top = jnp.max(s, axis=0, keepdims=True) * per_exp
            p = jnp.exp2(s * per_exp - top)
            dp = dot(win[at, 2 * width : 3 * width], d_out, NT)
            total = jnp.sum(p, axis=0, keepdims=True)
            weighted = jnp.sum(p * dp, axis=0, keepdims=True)
            column = j * query_rows + lax.broadcasted_iota(jnp.int32, (1, query_rows), 1)
            inverse = jnp.where((column >= head) & (column < tail), 1.0 / total, 0.0)
            p = p * inverse
            g = (p * (dp - weighted * inverse)).astype(jnp.bfloat16)
            acc_v[:key_rows, :] += dot(p.astype(jnp.bfloat16), grad, NN)
            acc_k[:key_rows, :] += dot(g, query, NN)
            new = (dot(keys_t[:, :key_rows], g, NN) * scaling).T
            row = j * query_rows + lax.broadcasted_iota(jnp.int32, (query_rows, width), 0)
            old = result[q_at, :width].astype(jnp.float32)
            result[q_at, :width] = jnp.where((row >= head) & (row < tail), new, old).astype(jnp.bfloat16)
            return 0

        lax.fori_loop(0, lax.div(tail + query_rows - 1, query_rows), query_tile, 0)
        values = acc_v[:key_rows, :]
        row = lax.broadcasted_iota(jnp.int32, (key_rows, width), 0)
        inside = (row >= head) & (row < tail)
        for n, new in ((1, acc_k[:key_rows, :] * scaling), (2, values * row_gate)):
            cols = slice(n * width, (n + 1) * width)
            old = result[at, cols].astype(jnp.float32)
            result[at, cols] = jnp.where(inside, new, old).astype(jnp.bfloat16)
        terms = values * win[at, 2 * width : 3 * width].astype(jnp.float32)
        gate_out[pl.ds(c, 1), :] = jnp.sum(terms, axis=0, keepdims=True)

    shapes = shapes_for(rows)
    origin = block * rows - pad

    def clip_step(c, _):
        start = starts[c] - origin
        base = pl.multiple_of(start // 16 * 16, 16)
        head = start - base
        tail = head + lengths[c]
        below = 0
        for key_rows, query_rows in shapes:

            @pl.when((tail > below) & (tail <= key_rows))
            def _():
                whole_clip(key_rows, query_rows, c, base, head, tail)

            below = key_rows
        return 0

    lax.fori_loop(clip_low, clip_high, clip_step, 0)

    last = pltpu.make_async_copy(result.at[pl.ds(pad, rows), :], own_out, sem.at[0])
    last.start()
    for j, at_row in places:
        slot = lax.rem(me + heads - j, heads)
        for r in range(heads):

            @pl.when(slot == r)
            def _():
                pltpu.make_async_copy(result.at[pl.ds(at_row, part), :], halo_outs[r], sem.at[1 + j]).start()
    last.wait()
    for j, at_row in places:
        pltpu.make_async_copy(result.at[pl.ds(at_row, part), :], halo_outs[0], sem.at[1 + j]).wait()


def shapes_for(rows):
    tile = rows // 4
    return [(n * tile, tile) for n in range(1, 5)] + [(rows + rows // 8, rows // 4 + rows // 8)]


def attention(place, lengths, own, halos, gate, heads, pad, width):
    rows = own.shape[0]
    part = rows // heads
    window = rows + 2 * pad
    spare = rows // 4
    anywhere = pl.BlockSpec(memory_space=pl.ANY)
    vmem = pl.BlockSpec(memory_space=pltpu.VMEM)
    smem = pl.BlockSpec(memory_space=pltpu.SMEM)
    geometry = (heads, rows, pad, width, width ** (-0.5))
    f32, b16 = jnp.float32, jnp.bfloat16
    most = shapes_for(rows)[-1][0]
    return pl.pallas_call(
        functools.partial(attention_kernel, geometry),
        out_shape=[jax.ShapeDtypeStruct((rows, 3 * width), b16)]
        + [jax.ShapeDtypeStruct((part, 3 * width), b16)] * heads
        + [jax.ShapeDtypeStruct(gate.shape, f32), jax.ShapeDtypeStruct((2,), jnp.int32)],
        in_specs=[smem] * 2 + [anywhere] * (1 + heads) + [vmem],
        out_specs=[anywhere] * (1 + heads) + [vmem, smem],
        scratch_shapes=[
            pltpu.VMEM((window + spare, 4 * width), b16),
            pltpu.VMEM((window + spare, 3 * width), b16),
            pltpu.VMEM((width, most), b16),
            pltpu.VMEM((most, width), f32),
            pltpu.VMEM((most, width), f32),
            pltpu.SMEM((gate.shape[0],), jnp.int32),
            pltpu.SemaphoreType.DMA((1 + heads,)),
        ],
        compiler_params=pltpu.CompilerParams(vmem_limit_bytes=48 * 1024 * 1024),
        cost_estimate=pl.CostEstimate(flops=4_000_000_000, bytes_accessed=4_000_000, transcendentals=4_000_000),
    )(place, lengths, own, *halos, gate)


def choose_kernel(heads, width, first_row, span, own, *refs):
    halos, outs = refs[:heads], refs[heads:]
    me = lax.axis_index("head")
    row = first_row[0] + lax.broadcasted_iota(jnp.int32, (own.shape[1], width), 0)
    keep = (row >= span[0]) & (row < span[1])
    for r in range(heads):
        head = lax.rem(me + r, heads)
        at = pl.ds(pl.multiple_of(head * width, width), width)
        kept, other = own[head].astype(jnp.float32), halos[r][...].astype(jnp.float32)
        for n, out in enumerate(outs):
            cols = slice(n * width, (n + 1) * width)
            out[:, at] = jnp.where(keep, kept[:, cols], other[:, cols]).astype(jnp.bfloat16)


def choose(first_row, span, own, halos, heads, width):
    part = own.shape[1]
    smem = pl.BlockSpec(memory_space=pltpu.SMEM)
    vmem = pl.BlockSpec(memory_space=pltpu.VMEM)
    return pl.pallas_call(
        functools.partial(choose_kernel, heads, width),
        out_shape=[jax.ShapeDtypeStruct((part, heads * width), jnp.bfloat16)] * 3,
        in_specs=[smem] * 2 + [vmem] * (1 + heads),
        out_specs=[vmem] * 3,
        compiler_params=pltpu.CompilerParams(vmem_limit_bytes=32 * 1024 * 1024),
    )(first_row, span, own, *halos)


def shards(heads, queries, token_keys, token_values, grad_out, clip_gate, clip_lengths):
    part, total_width = queries.shape
    width = total_width // heads
    rows = part * heads
    pad = rows // 2
    blocks = lax.axis_size("ctx")
    block, me = lax.axis_index("ctx"), lax.axis_index("head")

    packed, *sends = pack((queries, token_keys, token_values, grad_out), heads, width)
    own = lax.all_to_all(packed, "head", 0, 0, tiled=True).reshape(rows, 4 * width)
    halos = [lax.ppermute(sends[r], AXES, toward(r, blocks, heads)) for r in range(heads)]

    place = jnp.stack([block, me]).astype(jnp.int32)
    own_out, *rest = attention(
        place, clip_lengths, own, halos, clip_gate.astype(jnp.float32), heads, pad, width
    )
    halo_outs, gate_term, span = rest[:heads], rest[heads], rest[heads + 1]

    homes = [lax.ppermute(halo_outs[r], AXES, back(r, blocks, heads)) for r in range(heads)]
    mixed = lax.all_to_all(own_out.reshape(heads, part, 3 * width), "head", 0, 0, tiled=True)

    step = 1
    while step < blocks:
        gate_term = gate_term + lax.ppermute(gate_term, "ctx", [(i, i ^ step) for i in range(blocks)])
        step *= 2

    at = jnp.stack([rows * block + part * me]).astype(jnp.int32)
    grad_queries, grad_keys, grad_values = choose(at, span, mixed, homes, heads, width)
    return grad_queries, grad_keys, grad_values, gate_term


def solution(mesh):
    rows, columns = P(AXES, None), P(None, "head")
    return jax.shard_map(
        functools.partial(shards, mesh.shape["head"]),
        mesh=mesh,
        in_specs=(rows, rows, rows, rows, columns, P()),
        out_specs=(rows, rows, rows, columns),
        check_vma=False,
    )
```

```python
import functools
import math

import jax
import jax.numpy as jnp
from jax import lax
from jax.experimental import pallas as pl
from jax.experimental.pallas import tpu as pltpu
from jax.sharding import PartitionSpec as P

AXES = ("ctx", "head")
CHUNK = 256
STRIP = 128
NEG = -1e30
NT = (((1,), (1,)), ((), ()))
NN = (((1,), (0,)), ((), ()))


def dot(left, right, dims):
    return lax.dot_general(left, right, dims, preferred_element_type=jnp.float32)


def toward(shift, blocks, heads):
    pairs = []
    for i in range(blocks):
        for j in range(heads):
            target = i + 1 if j >= heads // 2 else i - 1
            if 0 <= target < blocks:
                pairs.append((i * heads + j, target * heads + (j + shift) % heads))
    return pairs


def back(shift, blocks, heads):
    return [(b, a) for a, b in toward(shift, blocks, heads)]


def pack_kernel(heads, width, *refs):
    arrays, packed, sends = refs[:4], refs[4], refs[5 : 5 + heads]
    held, sem = refs[5 + heads :]
    me = lax.axis_index("head")
    copies = [pltpu.make_async_copy(array, held.at[n], sem.at[n]) for n, array in enumerate(arrays)]
    for copy in copies:
        copy.start()
    for n, copy in enumerate(copies):
        copy.wait()
        cols = slice(n * width, (n + 1) * width)
        for h in range(heads):
            packed[h, :, cols] = held[n, :, h * width : (h + 1) * width]
        for r in range(heads):
            head = lax.rem(me + r, heads)
            sends[r][:, cols] = held[n, :, pl.ds(pl.multiple_of(head * width, width), width)]


def pack(arrays, heads, width):
    part = arrays[0].shape[0]
    one = jax.ShapeDtypeStruct((part, 4 * width), jnp.bfloat16)
    vmem = pl.BlockSpec(memory_space=pltpu.VMEM)
    return pl.pallas_call(
        functools.partial(pack_kernel, heads, width),
        out_shape=[jax.ShapeDtypeStruct((heads, part, 4 * width), jnp.bfloat16)] + [one] * heads,
        in_specs=[pl.BlockSpec(memory_space=pltpu.HBM)] * 4,
        out_specs=[vmem] * (1 + heads),
        scratch_shapes=[pltpu.VMEM((4, part, heads * width), jnp.bfloat16), pltpu.SemaphoreType.DMA((4,))],
        compiler_params=pltpu.CompilerParams(vmem_limit_bytes=60 * 1024 * 1024),
    )(*arrays)


def attention_kernel(geometry, place, lengths, own, *refs):
    heads, rows, pad, width, scaling = geometry
    part = rows // heads
    halos, refs = refs[:heads], refs[heads:]
    gate, own_out = refs[:2]
    halo_outs, refs = refs[2 : 2 + heads], refs[2 + heads :]
    gate_out, span_out, win, result, keys_t, acc_k, acc_v, weight, dprob, starts, sem = refs
    window = rows + 2 * pad
    per_exp = scaling * math.log2(math.e)
    block, me = place[0], place[1]
    clips = gate.shape[0]

    places = [(j, pad + rows + j * part if j < heads // 2 else (j - heads // 2) * part) for j in range(heads)]

    first = pltpu.make_async_copy(own, win.at[pl.ds(pad, rows), :], sem.at[0])
    first.start()
    for j, at_row in places:
        slot = lax.rem(me + heads - j, heads)
        for r in range(heads):

            @pl.when(slot == r)
            def _():
                pltpu.make_async_copy(halos[r], win.at[pl.ds(at_row, part), :], sem.at[1 + j]).start()

    def place_clip(c, carried):
        start, clip_low, clip_high, low, high = carried
        end = start + lengths[c]
        first_block, last_block = lax.div(start, rows), lax.div(end - 1, rows)
        edge = last_block * rows
        lower = (first_block != last_block) & (edge - start >= end - edge)
        owned = jnp.where(lower, first_block, last_block) == block
        starts[c] = start
        return (
            end,
            jnp.where(owned, jnp.minimum(clip_low, c), clip_low),
            jnp.where(owned, c + 1, clip_high),
            jnp.where(owned, jnp.minimum(low, start), low),
            jnp.where(owned, end, high),
        )

    most, zero = jnp.int32(2**30), jnp.int32(0)
    _, clip_low, clip_high, low, high = lax.fori_loop(0, clips, place_clip, (zero, most, zero, most, zero))
    span_out[0] = low
    span_out[1] = high
    gate_out[...] = jnp.zeros_like(gate_out)
    win[window:, :] = jnp.zeros((win.shape[0] - window, 4 * width), jnp.bfloat16)

    first.wait()
    for j, at_row in places:
        pltpu.make_async_copy(halos[0], win.at[pl.ds(at_row, part), :], sem.at[1 + j]).wait()

    def whole_clip(key_rows, query_rows, below, c, base, head, tail):
        at = pl.ds(base, key_rows)
        keys_t[:, :key_rows] = win[at, width : 2 * width].T
        acc_k[:key_rows, :] = jnp.zeros((key_rows, width), jnp.float32)
        acc_v[:key_rows, :] = jnp.zeros((key_rows, width), jnp.float32)
        row_gate = gate[pl.ds(c, 1), :]

        def query_tile(j, _):
            q_at = pl.ds(pl.multiple_of(base + j * query_rows, 16), query_rows)
            query, grad = win[q_at, :width], win[q_at, 3 * width :]
            d_out = (row_gate * grad.astype(jnp.float32)).astype(jnp.bfloat16)
            tops, totals, dots = [], [], []
            for k in range(0, key_rows, CHUNK):
                rows_k = min(CHUNK, key_rows - k)
                k_at = pl.ds(pl.multiple_of(base + k, 16), rows_k)
                s_all = dot(win[k_at, width : 2 * width], query, NT)
                dp_all = dot(win[k_at, 2 * width : 3 * width], d_out, NT)
                for m in range(0, rows_k, STRIP):
                    s, dp = s_all[m : m + STRIP], dp_all[m : m + STRIP]
                    if k + m < 16 or k + m + STRIP > below:
                        row = k + m + lax.broadcasted_iota(jnp.int32, s.shape, 0)
                        s = jnp.where((row >= head) & (row < tail), s, NEG)
                    top = jnp.max(s, axis=0, keepdims=True) * per_exp
                    p = jnp.exp2(s * per_exp - top)
                    weight[k + m : k + m + STRIP, :query_rows] = p
                    dprob[k + m : k + m + STRIP, :query_rows] = dp
                    tops.append(top)
                    totals.append(jnp.sum(p, axis=0, keepdims=True))
                    dots.append(jnp.sum(p * dp, axis=0, keepdims=True))
            top = functools.reduce(jnp.maximum, tops)
            scales = [jnp.exp2(t - top) for t in tops]
            total = sum(t * f for t, f in zip(totals, scales))
            weighted = sum(t * f for t, f in zip(dots, scales))
            column = j * query_rows + lax.broadcasted_iota(jnp.int32, (1, query_rows), 1)
            inverse = jnp.where((column >= head) & (column < tail), 1.0 / total, 0.0)
            row_dot = weighted * inverse
            probs, grads = [], []
            for n, f in enumerate(scales):
                at_n = slice(n * STRIP, (n + 1) * STRIP)
                p = weight[at_n, :query_rows] * (f * inverse)
                probs.append(p.astype(jnp.bfloat16))
                grads.append((p * (dprob[at_n, :query_rows] - row_dot)).astype(jnp.bfloat16))
            g = jnp.concatenate(grads, axis=0)
            acc_v[:key_rows, :] += dot(jnp.concatenate(probs, axis=0), grad, NN)
            acc_k[:key_rows, :] += dot(g, query, NN)
            new = (dot(keys_t[:, :key_rows], g, NN) * scaling).T
            row = j * query_rows + lax.broadcasted_iota(jnp.int32, (query_rows, width), 0)
            old = result[q_at, :width].astype(jnp.float32)
            result[q_at, :width] = jnp.where((row >= head) & (row < tail), new, old).astype(jnp.bfloat16)
            return 0

        lax.fori_loop(0, lax.div(tail + query_rows - 1, query_rows), query_tile, 0)
        values = acc_v[:key_rows, :]
        row = lax.broadcasted_iota(jnp.int32, (key_rows, width), 0)
        inside = (row >= head) & (row < tail)
        for n, new in ((1, acc_k[:key_rows, :] * scaling), (2, values * row_gate)):
            cols = slice(n * width, (n + 1) * width)
            old = result[at, cols].astype(jnp.float32)
            result[at, cols] = jnp.where(inside, new, old).astype(jnp.bfloat16)
        terms = values * win[at, 2 * width : 3 * width].astype(jnp.float32)
        gate_out[pl.ds(c, 1), :] = jnp.sum(terms, axis=0, keepdims=True)

    shapes = shapes_for(rows)
    origin = block * rows - pad

    def clip_step(c, _):
        start = starts[c] - origin
        base = pl.multiple_of(start // 16 * 16, 16)
        head = start - base
        tail = head + lengths[c]
        below = 0
        for key_rows, query_rows in shapes:

            @pl.when((tail > below) & (tail <= key_rows))
            def _(below=below):
                whole_clip(key_rows, query_rows, below, c, base, head, tail)

            below = key_rows
        return 0

    lax.fori_loop(clip_low, clip_high, clip_step, 0)

    last = pltpu.make_async_copy(result.at[pl.ds(pad, rows), :], own_out, sem.at[0])
    last.start()
    for j, at_row in places:
        slot = lax.rem(me + heads - j, heads)
        for r in range(heads):

            @pl.when(slot == r)
            def _():
                pltpu.make_async_copy(result.at[pl.ds(at_row, part), :], halo_outs[r], sem.at[1 + j]).start()
    last.wait()
    for j, at_row in places:
        pltpu.make_async_copy(result.at[pl.ds(at_row, part), :], halo_outs[0], sem.at[1 + j]).wait()


def shapes_for(rows):
    tile = rows // 4
    return [(n * tile, tile) for n in range(1, 5)] + [(rows + rows // 8, rows // 4 + rows // 8)]


def attention(place, lengths, own, halos, gate, heads, pad, width):
    rows = own.shape[0]
    part = rows // heads
    window = rows + 2 * pad
    spare = rows // 4
    anywhere = pl.BlockSpec(memory_space=pl.ANY)
    vmem = pl.BlockSpec(memory_space=pltpu.VMEM)
    smem = pl.BlockSpec(memory_space=pltpu.SMEM)
    geometry = (heads, rows, pad, width, width ** (-0.5))
    f32, b16 = jnp.float32, jnp.bfloat16
    most, widest = shapes_for(rows)[-1]
    return pl.pallas_call(
        functools.partial(attention_kernel, geometry),
        out_shape=[jax.ShapeDtypeStruct((rows, 3 * width), b16)]
        + [jax.ShapeDtypeStruct((part, 3 * width), b16)] * heads
        + [jax.ShapeDtypeStruct(gate.shape, f32), jax.ShapeDtypeStruct((2,), jnp.int32)],
        in_specs=[smem] * 2 + [anywhere] * (1 + heads) + [vmem],
        out_specs=[anywhere] * (1 + heads) + [vmem, smem],
        scratch_shapes=[
            pltpu.VMEM((window + spare, 4 * width), b16),
            pltpu.VMEM((window + spare, 3 * width), b16),
            pltpu.VMEM((width, most), b16),
            pltpu.VMEM((most, width), f32),
            pltpu.VMEM((most, width), f32),
            pltpu.VMEM((most, widest), f32),
            pltpu.VMEM((most, widest), f32),
            pltpu.SMEM((gate.shape[0],), jnp.int32),
            pltpu.SemaphoreType.DMA((1 + heads,)),
        ],
        compiler_params=pltpu.CompilerParams(vmem_limit_bytes=48 * 1024 * 1024),
        cost_estimate=pl.CostEstimate(flops=4_000_000_000, bytes_accessed=4_000_000, transcendentals=4_000_000),
    )(place, lengths, own, *halos, gate)


def choose_kernel(heads, width, first_row, span, own, *refs):
    halos, outs = refs[:heads], refs[heads:]
    me = lax.axis_index("head")
    row = first_row[0] + lax.broadcasted_iota(jnp.int32, (own.shape[1], width), 0)
    keep = (row >= span[0]) & (row < span[1])
    for r in range(heads):
        head = lax.rem(me + r, heads)
        at = pl.ds(pl.multiple_of(head * width, width), width)
        kept, other = own[head].astype(jnp.float32), halos[r][...].astype(jnp.float32)
        for n, out in enumerate(outs):
            cols = slice(n * width, (n + 1) * width)
            out[:, at] = jnp.where(keep, kept[:, cols], other[:, cols]).astype(jnp.bfloat16)


def choose(first_row, span, own, halos, heads, width):
    part = own.shape[1]
    smem = pl.BlockSpec(memory_space=pltpu.SMEM)
    vmem = pl.BlockSpec(memory_space=pltpu.VMEM)
    return pl.pallas_call(
        functools.partial(choose_kernel, heads, width),
        out_shape=[jax.ShapeDtypeStruct((part, heads * width), jnp.bfloat16)] * 3,
        in_specs=[smem] * 2 + [vmem] * (1 + heads),
        out_specs=[vmem] * 3,
        compiler_params=pltpu.CompilerParams(vmem_limit_bytes=32 * 1024 * 1024),
    )(first_row, span, own, *halos)


def shards(heads, queries, token_keys, token_values, grad_out, clip_gate, clip_lengths):
    part, total_width = queries.shape
    width = total_width // heads
    rows = part * heads
    pad = rows // 2
    blocks = lax.axis_size("ctx")
    block, me = lax.axis_index("ctx"), lax.axis_index("head")

    packed, *sends = pack((queries, token_keys, token_values, grad_out), heads, width)
    own = lax.all_to_all(packed, "head", 0, 0, tiled=True).reshape(rows, 4 * width)
    halos = [lax.ppermute(sends[r], AXES, toward(r, blocks, heads)) for r in range(heads)]

    place = jnp.stack([block, me]).astype(jnp.int32)
    own_out, *rest = attention(
        place, clip_lengths, own, halos, clip_gate.astype(jnp.float32), heads, pad, width
    )
    halo_outs, gate_term, span = rest[:heads], rest[heads], rest[heads + 1]

    gate_term = gate_term + lax.ppermute(gate_term, "ctx", [(i, i ^ 1) for i in range(blocks)])
    gate_term = gate_term + lax.ppermute(gate_term, "ctx", [(i, i ^ 2) for i in range(blocks)])
    halo_outs[1], halo_outs[2], halo_outs[3], gate_term = lax.optimization_barrier((halo_outs[1], halo_outs[2], halo_outs[3], gate_term))
    step = 4
    while step < blocks:
        gate_term = gate_term + lax.ppermute(gate_term, "ctx", [(i, i ^ step) for i in range(blocks)])
        step *= 2
    mixed = lax.all_to_all(own_out.reshape(heads, part, 3 * width), "head", 0, 0, tiled=True)
    homes = [lax.ppermute(halo_outs[r], AXES, back(r, blocks, heads)) for r in range(heads)]

    at = jnp.stack([rows * block + part * me]).astype(jnp.int32)
    grad_queries, grad_keys, grad_values = choose(at, span, mixed, homes, heads, width)
    return grad_queries, grad_keys, grad_values, gate_term


def solution(mesh):
    rows, columns = P(AXES, None), P(None, "head")
    return jax.shard_map(
        functools.partial(shards, mesh.shape["head"]),
        mesh=mesh,
        in_specs=(rows, rows, rows, rows, columns, P()),
        out_specs=(rows, rows, rows, columns),
        check_vma=False,
    )
```

```python
import functools
import itertools
import math

import jax
import jax.numpy as jnp
from jax import lax
from jax.experimental import pallas as pl
from jax.experimental.pallas import tpu as pltpu
from jax.sharding import PartitionSpec as P

AXES = ("ctx", "head")
CHUNK = 256
STRIP = 128
NEG = -1e30
NT = (((1,), (1,)), ((), ()))
NN = (((1,), (0,)), ((), ()))


def dot(left, right, dims):
    return lax.dot_general(left, right, dims, preferred_element_type=jnp.float32)


def toward(shift, blocks, heads):
    pairs = []
    for i in range(blocks):
        for j in range(heads):
            target = i + 1 if j >= heads // 2 else i - 1
            if 0 <= target < blocks:
                pairs.append((i * heads + j, target * heads + (j + shift) % heads))
    return pairs


def back(shift, blocks, heads):
    return [(b, a) for a, b in toward(shift, blocks, heads)]


def pack_kernel(heads, width, *refs):
    arrays, packed, sends = refs[:4], refs[4], refs[5 : 5 + heads]
    held, sem = refs[5 + heads :]
    me = lax.axis_index("head")
    copies = [pltpu.make_async_copy(array, held.at[n], sem.at[n]) for n, array in enumerate(arrays)]
    for copy in copies:
        copy.start()
    for n, copy in enumerate(copies):
        copy.wait()
        cols = slice(n * width, (n + 1) * width)
        for h in range(heads):
            packed[h, :, cols] = held[n, :, h * width : (h + 1) * width]
        for r in range(heads):
            head = lax.rem(me + r, heads)
            sends[r][:, cols] = held[n, :, pl.ds(pl.multiple_of(head * width, width), width)]


def pack(arrays, heads, width):
    part = arrays[0].shape[0]
    one = jax.ShapeDtypeStruct((part, 4 * width), jnp.bfloat16)
    vmem = pl.BlockSpec(memory_space=pltpu.VMEM)
    return pl.pallas_call(
        functools.partial(pack_kernel, heads, width),
        out_shape=[jax.ShapeDtypeStruct((heads, part, 4 * width), jnp.bfloat16)] + [one] * heads,
        in_specs=[pl.BlockSpec(memory_space=pltpu.HBM)] * 4,
        out_specs=[vmem] * (1 + heads),
        scratch_shapes=[pltpu.VMEM((4, part, heads * width), jnp.bfloat16), pltpu.SemaphoreType.DMA((4,))],
        compiler_params=pltpu.CompilerParams(vmem_limit_bytes=60 * 1024 * 1024),
    )(*arrays)


def attention_kernel(geometry, place, lengths, own, *refs):
    heads, rows, pad, width, scaling = geometry
    part = rows // heads
    halos, refs = refs[:heads], refs[heads:]
    gate, own_out = refs[:2]
    halo_outs, refs = refs[2 : 2 + heads], refs[2 + heads :]
    gate_out, span_out, win, result, keys_t, acc_k, acc_v, *held, starts, sem = refs
    window = rows + 2 * pad
    per_exp = scaling * math.log2(math.e)
    block, me = place[0], place[1]
    clips = gate.shape[0]

    places = [(j, pad + rows + j * part if j < heads // 2 else (j - heads // 2) * part) for j in range(heads)]

    first = pltpu.make_async_copy(own, win.at[pl.ds(pad, rows), :], sem.at[0])
    first.start()
    for j, at_row in places:
        slot = lax.rem(me + heads - j, heads)
        for r in range(heads):

            @pl.when(slot == r)
            def _():
                pltpu.make_async_copy(halos[r], win.at[pl.ds(at_row, part), :], sem.at[1 + j]).start()

    def place_clip(c, carried):
        start, clip_low, clip_high, low, high = carried
        end = start + lengths[c]
        first_block, last_block = lax.div(start, rows), lax.div(end - 1, rows)
        edge = last_block * rows
        lower = (first_block != last_block) & (edge - start >= end - edge)
        owned = jnp.where(lower, first_block, last_block) == block
        starts[c] = start
        return (
            end,
            jnp.where(owned, jnp.minimum(clip_low, c), clip_low),
            jnp.where(owned, c + 1, clip_high),
            jnp.where(owned, jnp.minimum(low, start), low),
            jnp.where(owned, end, high),
        )

    most, zero = jnp.int32(2**30), jnp.int32(0)
    _, clip_low, clip_high, low, high = lax.fori_loop(0, clips, place_clip, (zero, most, zero, most, zero))
    span_out[0] = low
    span_out[1] = high
    gate_out[...] = jnp.zeros_like(gate_out)
    win[window:, :] = jnp.zeros((win.shape[0] - window, 4 * width), jnp.bfloat16)

    first.wait()
    for j, at_row in places:
        pltpu.make_async_copy(halos[0], win.at[pl.ds(at_row, part), :], sem.at[1 + j]).wait()

    def whole_clip(key_rows, query_rows, below, c, base, head, tail):
        at = pl.ds(base, key_rows)
        keys_t[:, :key_rows] = win[at, width : 2 * width].T
        row_gate = gate[pl.ds(c, 1), :]

        def scores(j):
            q_at = pl.ds(pl.multiple_of(base + j * query_rows, 16), query_rows)
            query, grad = win[q_at, :width], win[q_at, 3 * width :]
            d_out = (row_gate * grad.astype(jnp.float32)).astype(jnp.bfloat16)
            weight, dprob = held[2 * (j % 2)], held[2 * (j % 2) + 1]
            tops, totals, dots = [], [], []
            for k in range(0, key_rows, CHUNK):
                rows_k = min(CHUNK, key_rows - k)
                k_at = pl.ds(pl.multiple_of(base + k, 16), rows_k)
                s_all = dot(win[k_at, width : 2 * width], query, NT)
                dp_all = dot(win[k_at, 2 * width : 3 * width], d_out, NT)
                for m in range(0, rows_k, STRIP):
                    s, dp = s_all[m : m + STRIP], dp_all[m : m + STRIP]
                    if k + m < 16 or k + m + STRIP > below:
                        row = k + m + lax.broadcasted_iota(jnp.int32, s.shape, 0)
                        s = jnp.where((row >= head) & (row < tail), s, NEG)
                    top = jnp.max(s, axis=0, keepdims=True) * per_exp
                    p = jnp.exp2(s * per_exp - top)
                    weight[k + m : k + m + STRIP, :query_rows] = p
                    dprob[k + m : k + m + STRIP, :query_rows] = dp
                    tops.append(top)
                    totals.append(jnp.sum(p, axis=0, keepdims=True))
                    dots.append(jnp.sum(p * dp, axis=0, keepdims=True))
                yield None
            top = functools.reduce(jnp.maximum, tops)
            scales = [jnp.exp2(t - top) for t in tops]
            total = sum(t * f for t, f in zip(totals, scales))
            weighted = sum(t * f for t, f in zip(dots, scales))
            column = j * query_rows + lax.broadcasted_iota(jnp.int32, (1, query_rows), 1)
            inverse = jnp.where((column >= head) & (column < tail), 1.0 / total, 0.0)
            yield j, q_at, [f * inverse for f in scales], weighted * inverse

        def gradients(state):
            j, q_at, scales, row_dot = state
            query, grad = win[q_at, :width], win[q_at, 3 * width :]
            weight, dprob = held[2 * (j % 2)], held[2 * (j % 2) + 1]
            kept = []
            for k in range(0, key_rows, CHUNK):
                upto = min(k + CHUNK, key_rows)
                probs, grads = [], []
                for m in range(k, upto, STRIP):
                    p = weight[m : m + STRIP, :query_rows] * scales[m // STRIP]
                    probs.append(p.astype(jnp.bfloat16))
                    grads.append((p * (dprob[m : m + STRIP, :query_rows] - row_dot)).astype(jnp.bfloat16))
                p, g = jnp.concatenate(probs, axis=0), jnp.concatenate(grads, axis=0)
                kept.append(g)
                for acc, term in ((acc_v, dot(p, grad, NN)), (acc_k, dot(g, query, NN))):
                    acc[k:upto, :] = term if j == 0 else acc[k:upto, :] + term
                yield None
            new = (dot(keys_t[:, :key_rows], jnp.concatenate(kept, axis=0), NN) * scaling).T
            row = j * query_rows + lax.broadcasted_iota(jnp.int32, (query_rows, width), 0)
            old = result[q_at, :width].astype(jnp.float32)
            result[q_at, :width] = jnp.where((row >= head) & (row < tail), new, old).astype(jnp.bfloat16)
            yield None

        state = None
        for j in range(-(-key_rows // query_rows) + 1):
            ahead = scores(j) if j * query_rows < key_rows else iter(())
            behind = gradients(state) if j > 0 else iter(())
            for state, _ in itertools.zip_longest(ahead, behind):
                pass

        values = acc_v[:key_rows, :]
        row = lax.broadcasted_iota(jnp.int32, (key_rows, width), 0)
        inside = (row >= head) & (row < tail)
        for n, new in ((1, acc_k[:key_rows, :] * scaling), (2, values * row_gate)):
            cols = slice(n * width, (n + 1) * width)
            old = result[at, cols].astype(jnp.float32)
            result[at, cols] = jnp.where(inside, new, old).astype(jnp.bfloat16)
        terms = values * win[at, 2 * width : 3 * width].astype(jnp.float32)
        gate_out[pl.ds(c, 1), :] = jnp.sum(terms, axis=0, keepdims=True)

    shapes = shapes_for(rows)
    origin = block * rows - pad

    def clip_step(c, _):
        start = starts[c] - origin
        base = pl.multiple_of(start // 16 * 16, 16)
        head = start - base
        tail = head + lengths[c]
        below = 0
        for key_rows, query_rows in shapes:

            @pl.when((tail > below) & (tail <= key_rows))
            def _(below=below):
                whole_clip(key_rows, query_rows, below, c, base, head, tail)

            below = key_rows
        return 0

    lax.fori_loop(clip_low, clip_high, clip_step, 0)

    last = pltpu.make_async_copy(result.at[pl.ds(pad, rows), :], own_out, sem.at[0])
    last.start()
    for j, at_row in places:
        slot = lax.rem(me + heads - j, heads)
        for r in range(heads):

            @pl.when(slot == r)
            def _():
                pltpu.make_async_copy(result.at[pl.ds(at_row, part), :], halo_outs[r], sem.at[1 + j]).start()
    last.wait()
    for j, at_row in places:
        pltpu.make_async_copy(result.at[pl.ds(at_row, part), :], halo_outs[0], sem.at[1 + j]).wait()


def shapes_for(rows):
    tile = rows // 4
    return [(n * tile, tile) for n in range(1, 5)] + [(rows + rows // 8, rows // 4 + rows // 8)]


def attention(place, lengths, own, halos, gate, heads, pad, width):
    rows = own.shape[0]
    part = rows // heads
    window = rows + 2 * pad
    spare = rows // 4
    anywhere = pl.BlockSpec(memory_space=pl.ANY)
    vmem = pl.BlockSpec(memory_space=pltpu.VMEM)
    smem = pl.BlockSpec(memory_space=pltpu.SMEM)
    geometry = (heads, rows, pad, width, width ** (-0.5))
    f32, b16 = jnp.float32, jnp.bfloat16
    most, widest = shapes_for(rows)[-1]
    return pl.pallas_call(
        functools.partial(attention_kernel, geometry),
        out_shape=[jax.ShapeDtypeStruct((rows, 3 * width), b16)]
        + [jax.ShapeDtypeStruct((part, 3 * width), b16)] * heads
        + [jax.ShapeDtypeStruct(gate.shape, f32), jax.ShapeDtypeStruct((2,), jnp.int32)],
        in_specs=[smem] * 2 + [anywhere] * (1 + heads) + [vmem],
        out_specs=[anywhere] * (1 + heads) + [vmem, smem],
        scratch_shapes=[
            pltpu.VMEM((window + spare, 4 * width), b16),
            pltpu.VMEM((window + spare, 3 * width), b16),
            pltpu.VMEM((width, most), b16),
            pltpu.VMEM((most, width), f32),
            pltpu.VMEM((most, width), f32),
            *[pltpu.VMEM((most, widest), f32)] * 4,
            pltpu.SMEM((gate.shape[0],), jnp.int32),
            pltpu.SemaphoreType.DMA((1 + heads,)),
        ],
        compiler_params=pltpu.CompilerParams(vmem_limit_bytes=48 * 1024 * 1024),
        cost_estimate=pl.CostEstimate(flops=4_000_000_000, bytes_accessed=4_000_000, transcendentals=4_000_000),
    )(place, lengths, own, *halos, gate)


def choose_kernel(heads, width, first_row, span, own, *refs):
    halos, outs = refs[:heads], refs[heads:]
    me = lax.axis_index("head")
    row = first_row[0] + lax.broadcasted_iota(jnp.int32, (own.shape[1], width), 0)
    keep = (row >= span[0]) & (row < span[1])
    for r in range(heads):
        head = lax.rem(me + r, heads)
        at = pl.ds(pl.multiple_of(head * width, width), width)
        kept, other = own[head].astype(jnp.float32), halos[r][...].astype(jnp.float32)
        for n, out in enumerate(outs):
            cols = slice(n * width, (n + 1) * width)
            out[:, at] = jnp.where(keep, kept[:, cols], other[:, cols]).astype(jnp.bfloat16)


def choose(first_row, span, own, halos, heads, width):
    part = own.shape[1]
    smem = pl.BlockSpec(memory_space=pltpu.SMEM)
    vmem = pl.BlockSpec(memory_space=pltpu.VMEM)
    return pl.pallas_call(
        functools.partial(choose_kernel, heads, width),
        out_shape=[jax.ShapeDtypeStruct((part, heads * width), jnp.bfloat16)] * 3,
        in_specs=[smem] * 2 + [vmem] * (1 + heads),
        out_specs=[vmem] * 3,
        compiler_params=pltpu.CompilerParams(vmem_limit_bytes=32 * 1024 * 1024),
    )(first_row, span, own, *halos)


def shards(heads, queries, token_keys, token_values, grad_out, clip_gate, clip_lengths):
    part, total_width = queries.shape
    width = total_width // heads
    rows = part * heads
    pad = rows // 2
    blocks = lax.axis_size("ctx")
    block, me = lax.axis_index("ctx"), lax.axis_index("head")

    packed, *sends = pack((queries, token_keys, token_values, grad_out), heads, width)
    own = lax.all_to_all(packed, "head", 0, 0, tiled=True).reshape(rows, 4 * width)
    halos = [lax.ppermute(sends[r], AXES, toward(r, blocks, heads)) for r in range(heads)]

    place = jnp.stack([block, me]).astype(jnp.int32)
    own_out, *rest = attention(
        place, clip_lengths, own, halos, clip_gate.astype(jnp.float32), heads, pad, width
    )
    halo_outs, gate_term, span = rest[:heads], rest[heads], rest[heads + 1]

    gate_term = gate_term + lax.ppermute(gate_term, "ctx", [(i, i ^ 1) for i in range(blocks)])
    gate_term = gate_term + lax.ppermute(gate_term, "ctx", [(i, i ^ 2) for i in range(blocks)])
    halo_outs[1], halo_outs[2], halo_outs[3], gate_term = lax.optimization_barrier((halo_outs[1], halo_outs[2], halo_outs[3], gate_term))
    step = 4
    while step < blocks:
        gate_term = gate_term + lax.ppermute(gate_term, "ctx", [(i, i ^ step) for i in range(blocks)])
        step *= 2
    mixed = lax.all_to_all(own_out.reshape(heads, part, 3 * width), "head", 0, 0, tiled=True)
    homes = [lax.ppermute(halo_outs[r], AXES, back(r, blocks, heads)) for r in range(heads)]

    at = jnp.stack([rows * block + part * me]).astype(jnp.int32)
    grad_queries, grad_keys, grad_values = choose(at, span, mixed, homes, heads, width)
    return grad_queries, grad_keys, grad_values, gate_term


def solution(mesh):
    rows, columns = P(AXES, None), P(None, "head")
    return jax.shard_map(
        functools.partial(shards, mesh.shape["head"]),
        mesh=mesh,
        in_specs=(rows, rows, rows, rows, columns, P()),
        out_specs=(rows, rows, rows, columns),
        check_vma=False,
    )
```

```python
import functools
import itertools
import math

import jax
import jax.numpy as jnp
from jax import lax
from jax.experimental import pallas as pl
from jax.experimental.pallas import tpu as pltpu
from jax.sharding import PartitionSpec as P

AXES = ("ctx", "head")
CHUNK = 256
STRIP = 128
NEG = -1e30
NT = (((1,), (1,)), ((), ()))
NN = (((1,), (0,)), ((), ()))


def dot(left, right, dims):
    return lax.dot_general(left, right, dims, preferred_element_type=jnp.float32)


def toward(shift, blocks, heads):
    pairs = []
    for i in range(blocks):
        for j in range(heads):
            target = i + 1 if j >= heads // 2 else i - 1
            if 0 <= target < blocks:
                pairs.append((i * heads + j, target * heads + (j + shift) % heads))
    return pairs


def back(shift, blocks, heads):
    return [(b, a) for a, b in toward(shift, blocks, heads)]


def pack_kernel(heads, width, *refs):
    arrays, packed, sends = refs[:4], refs[4], refs[5 : 5 + heads]
    held, sem = refs[5 + heads :]
    me = lax.axis_index("head")
    copies = [pltpu.make_async_copy(array, held.at[n], sem.at[n]) for n, array in enumerate(arrays)]
    for copy in copies:
        copy.start()
    for n, copy in enumerate(copies):
        copy.wait()
        cols = slice(n * width, (n + 1) * width)
        for h in range(heads):
            packed[h, :, cols] = held[n, :, h * width : (h + 1) * width]
        for r in range(heads):
            head = lax.rem(me + r, heads)
            sends[r][:, cols] = held[n, :, pl.ds(pl.multiple_of(head * width, width), width)]


def pack(arrays, heads, width):
    part = arrays[0].shape[0]
    one = jax.ShapeDtypeStruct((part, 4 * width), jnp.bfloat16)
    vmem = pl.BlockSpec(memory_space=pltpu.VMEM)
    return pl.pallas_call(
        functools.partial(pack_kernel, heads, width),
        out_shape=[jax.ShapeDtypeStruct((heads, part, 4 * width), jnp.bfloat16)] + [one] * heads,
        in_specs=[pl.BlockSpec(memory_space=pltpu.HBM)] * 4,
        out_specs=[vmem] * (1 + heads),
        scratch_shapes=[pltpu.VMEM((4, part, heads * width), jnp.bfloat16), pltpu.SemaphoreType.DMA((4,))],
        compiler_params=pltpu.CompilerParams(vmem_limit_bytes=60 * 1024 * 1024),
    )(*arrays)


def attention_kernel(geometry, place, lengths, own, *refs):
    heads, rows, pad, width, scaling = geometry
    part = rows // heads
    halos, refs = refs[:heads], refs[heads:]
    gate, own_out = refs[:2]
    halo_outs, refs = refs[2 : 2 + heads], refs[2 + heads :]
    gate_out, span_out, win, result, keys_t, acc_k, acc_v, *held, starts, sem = refs
    window = rows + 2 * pad
    per_exp = scaling * math.log2(math.e)
    block, me = place[0], place[1]
    clips = gate.shape[0]

    places = [(j, pad + rows + j * part if j < heads // 2 else (j - heads // 2) * part) for j in range(heads)]

    first = pltpu.make_async_copy(own, win.at[pl.ds(pad, rows), :], sem.at[0])
    first.start()
    for j, at_row in places:
        slot = lax.rem(me + heads - j, heads)
        for r in range(heads):

            @pl.when(slot == r)
            def _():
                pltpu.make_async_copy(halos[r], win.at[pl.ds(at_row, part), :], sem.at[1 + j]).start()

    def place_clip(c, carried):
        start, clip_low, clip_high, low, high = carried
        end = start + lengths[c]
        first_block, last_block = lax.div(start, rows), lax.div(end - 1, rows)
        edge = last_block * rows
        lower = (first_block != last_block) & (edge - start >= end - edge)
        owned = jnp.where(lower, first_block, last_block) == block
        starts[c] = start
        return (
            end,
            jnp.where(owned, jnp.minimum(clip_low, c), clip_low),
            jnp.where(owned, c + 1, clip_high),
            jnp.where(owned, jnp.minimum(low, start), low),
            jnp.where(owned, end, high),
        )

    most, zero = jnp.int32(2**30), jnp.int32(0)
    _, clip_low, clip_high, low, high = lax.fori_loop(0, clips, place_clip, (zero, most, zero, most, zero))
    span_out[0] = low
    span_out[1] = high
    gate_out[...] = jnp.zeros_like(gate_out)
    win[window:, :] = jnp.zeros((win.shape[0] - window, 4 * width), jnp.bfloat16)

    first.wait()
    for j, at_row in places:
        pltpu.make_async_copy(halos[0], win.at[pl.ds(at_row, part), :], sem.at[1 + j]).wait()

    def whole_clip(key_rows, query_rows, below, c, base, head, tail):
        at = pl.ds(base, key_rows)
        keys_t[:, :key_rows] = win[at, width : 2 * width].T
        row_gate = gate[pl.ds(c, 1), :]

        def scores(j):
            q_at = pl.ds(pl.multiple_of(base + j * query_rows, 16), query_rows)
            query, grad = win[q_at, :width], win[q_at, 3 * width :]
            d_out = (row_gate * grad.astype(jnp.float32)).astype(jnp.bfloat16)
            weight, dprob = held[2 * (j % 2)], held[2 * (j % 2) + 1]
            tops, totals, dots = [], [], []
            for k in range(0, key_rows, CHUNK):
                rows_k = min(CHUNK, key_rows - k)
                k_at = pl.ds(pl.multiple_of(base + k, 16), rows_k)
                s_all = dot(win[k_at, width : 2 * width], query, NT)
                dp_all = dot(win[k_at, 2 * width : 3 * width], d_out, NT)
                for m in range(0, rows_k, STRIP):
                    s, dp = s_all[m : m + STRIP], dp_all[m : m + STRIP]
                    if k + m < 16 or k + m + STRIP > below:
                        row = k + m + lax.broadcasted_iota(jnp.int32, s.shape, 0)
                        s = jnp.where((row >= head) & (row < tail), s, NEG)
                    top = jnp.max(s, axis=0, keepdims=True) * per_exp
                    p = jnp.exp2(s * per_exp - top)
                    weight[k + m : k + m + STRIP, :query_rows] = p
                    dprob[k + m : k + m + STRIP, :query_rows] = dp
                    tops.append(top)
                    totals.append(jnp.sum(p, axis=0, keepdims=True))
                    dots.append(jnp.sum(p * dp, axis=0, keepdims=True))
                yield None
            top = functools.reduce(jnp.maximum, tops)
            scales = [jnp.exp2(t - top) for t in tops]
            total = sum(t * f for t, f in zip(totals, scales))
            weighted = sum(t * f for t, f in zip(dots, scales))
            column = j * query_rows + lax.broadcasted_iota(jnp.int32, (1, query_rows), 1)
            inverse = jnp.where((column >= head) & (column < tail), 1.0 / total, 0.0)
            yield j, q_at, [f * inverse for f in scales], weighted * inverse

        def gradients(state):
            j, q_at, scales, row_dot = state
            query, grad = win[q_at, :width], win[q_at, 3 * width :]
            weight, dprob = held[2 * (j % 2)], held[2 * (j % 2) + 1]
            kept = []
            for k in range(0, key_rows, CHUNK):
                upto = min(k + CHUNK, key_rows)
                probs, grads = [], []
                for m in range(k, upto, STRIP):
                    p = weight[m : m + STRIP, :query_rows] * scales[m // STRIP]
                    probs.append(p.astype(jnp.bfloat16))
                    grads.append((p * (dprob[m : m + STRIP, :query_rows] - row_dot)).astype(jnp.bfloat16))
                p, g = jnp.concatenate(probs, axis=0), jnp.concatenate(grads, axis=0)
                kept.append(g)
                for acc, term in ((acc_v, dot(p, grad, NN)), (acc_k, dot(g, query, NN))):
                    acc[k:upto, :] = term if j == 0 else acc[k:upto, :] + term
                yield None
            new = (dot(keys_t[:, :key_rows], jnp.concatenate(kept, axis=0), NN) * scaling).T
            row = j * query_rows + lax.broadcasted_iota(jnp.int32, (query_rows, width), 0)
            old = result[q_at, :width].astype(jnp.float32)
            result[q_at, :width] = jnp.where((row >= head) & (row < tail), new, old).astype(jnp.bfloat16)
            yield None

        state = None
        for j in range(-(-key_rows // query_rows) + 1):
            ahead = scores(j) if j * query_rows < key_rows else iter(())
            behind = gradients(state) if j > 0 else iter(())
            for state, _ in itertools.zip_longest(ahead, behind):
                pass

        values = acc_v[:key_rows, :]
        row = lax.broadcasted_iota(jnp.int32, (key_rows, width), 0)
        inside = (row >= head) & (row < tail)
        for n, new in ((1, acc_k[:key_rows, :] * scaling), (2, values * row_gate)):
            cols = slice(n * width, (n + 1) * width)
            old = result[at, cols].astype(jnp.float32)
            result[at, cols] = jnp.where(inside, new, old).astype(jnp.bfloat16)
        terms = values * win[at, 2 * width : 3 * width].astype(jnp.float32)
        gate_out[pl.ds(c, 1), :] = jnp.sum(terms, axis=0, keepdims=True)

    shapes = shapes_for(rows)
    origin = block * rows - pad

    def clip_step(c, _):
        start = starts[c] - origin
        base = pl.multiple_of(start // 16 * 16, 16)
        head = start - base
        tail = head + lengths[c]
        below = 0
        for key_rows, query_rows in shapes:

            @pl.when((tail > below) & (tail <= key_rows))
            def _(below=below):
                whole_clip(key_rows, query_rows, below, c, base, head, tail)

            below = key_rows
        return 0

    lax.fori_loop(clip_low, clip_high, clip_step, 0)

    last = pltpu.make_async_copy(result.at[pl.ds(pad, rows), :], own_out, sem.at[0])
    last.start()
    for j, at_row in places:
        slot = lax.rem(me + heads - j, heads)
        for r in range(heads):

            @pl.when(slot == r)
            def _():
                pltpu.make_async_copy(result.at[pl.ds(at_row, part), :], halo_outs[r], sem.at[1 + j]).start()
    last.wait()
    for j, at_row in places:
        pltpu.make_async_copy(result.at[pl.ds(at_row, part), :], halo_outs[0], sem.at[1 + j]).wait()


def shapes_for(rows):
    tile = rows // 4
    return [(n * tile, tile) for n in range(1, 5)] + [(rows + rows // 8, rows // 4 + rows // 8)]


def attention(place, lengths, own, halos, gate, heads, pad, width):
    rows = own.shape[0]
    part = rows // heads
    window = rows + 2 * pad
    spare = rows // 4
    anywhere = pl.BlockSpec(memory_space=pl.ANY)
    vmem = pl.BlockSpec(memory_space=pltpu.VMEM)
    smem = pl.BlockSpec(memory_space=pltpu.SMEM)
    geometry = (heads, rows, pad, width, width ** (-0.5))
    f32, b16 = jnp.float32, jnp.bfloat16
    most, widest = shapes_for(rows)[-1]
    return pl.pallas_call(
        functools.partial(attention_kernel, geometry),
        out_shape=[jax.ShapeDtypeStruct((rows, 3 * width), b16)]
        + [jax.ShapeDtypeStruct((part, 3 * width), b16)] * heads
        + [jax.ShapeDtypeStruct(gate.shape, f32), jax.ShapeDtypeStruct((2,), jnp.int32)],
        in_specs=[smem] * 2 + [anywhere] * (1 + heads) + [vmem],
        out_specs=[anywhere] * (1 + heads) + [vmem, smem],
        scratch_shapes=[
            pltpu.VMEM((window + spare, 4 * width), b16),
            pltpu.VMEM((window + spare, 3 * width), b16),
            pltpu.VMEM((width, most), b16),
            pltpu.VMEM((most, width), f32),
            pltpu.VMEM((most, width), f32),
            *[pltpu.VMEM((most, widest), f32)] * 4,
            pltpu.SMEM((gate.shape[0],), jnp.int32),
            pltpu.SemaphoreType.DMA((1 + heads,)),
        ],
        compiler_params=pltpu.CompilerParams(vmem_limit_bytes=48 * 1024 * 1024),
        cost_estimate=pl.CostEstimate(flops=4_000_000_000, bytes_accessed=4_000_000, transcendentals=4_000_000),
    )(place, lengths, own, *halos, gate)


def choose_kernel(heads, width, first_row, span, own, *refs):
    halos, outs = refs[:heads], refs[heads:]
    me = lax.axis_index("head")
    row = first_row[0] + lax.broadcasted_iota(jnp.int32, (own.shape[1], width), 0)
    keep = (row >= span[0]) & (row < span[1])
    for r in range(heads):
        head = lax.rem(me + r, heads)
        at = pl.ds(pl.multiple_of(head * width, width), width)
        kept, other = own[head].astype(jnp.float32), halos[r][...].astype(jnp.float32)
        for n, out in enumerate(outs):
            cols = slice(n * width, (n + 1) * width)
            out[:, at] = jnp.where(keep, kept[:, cols], other[:, cols]).astype(jnp.bfloat16)


def choose(first_row, span, own, halos, heads, width):
    part = own.shape[1]
    smem = pl.BlockSpec(memory_space=pltpu.SMEM)
    vmem = pl.BlockSpec(memory_space=pltpu.VMEM)
    return pl.pallas_call(
        functools.partial(choose_kernel, heads, width),
        out_shape=[jax.ShapeDtypeStruct((part, heads * width), jnp.bfloat16)] * 3,
        in_specs=[smem] * 2 + [vmem] * (1 + heads),
        out_specs=[vmem] * 3,
        compiler_params=pltpu.CompilerParams(vmem_limit_bytes=32 * 1024 * 1024),
    )(first_row, span, own, *halos)


def shards(heads, queries, token_keys, token_values, grad_out, clip_gate, clip_lengths):
    part, total_width = queries.shape
    width = total_width // heads
    rows = part * heads
    pad = rows // 2
    blocks = lax.axis_size("ctx")
    block, me = lax.axis_index("ctx"), lax.axis_index("head")

    packed, *sends = pack((queries, token_keys, token_values, grad_out), heads, width)
    own = lax.all_to_all(packed, "head", 0, 0, tiled=True).reshape(rows, 4 * width)
    halos = [lax.ppermute(sends[r], AXES, toward(r, blocks, heads)) for r in range(heads)]

    place = jnp.stack([block, me]).astype(jnp.int32)
    own_out, *rest = attention(
        place, clip_lengths, own, halos, clip_gate.astype(jnp.float32), heads, pad, width
    )
    halo_outs, gate_term, span = rest[:heads], rest[heads], rest[heads + 1]

    gate_term = gate_term + lax.ppermute(gate_term, "ctx", [(i, i ^ 1) for i in range(blocks)])
    gate_term = gate_term + lax.ppermute(gate_term, "ctx", [(i, i ^ 2) for i in range(blocks)])
    halo_outs[1], halo_outs[3], gate_term = lax.optimization_barrier((halo_outs[1], halo_outs[3], gate_term))
    step = 4
    while step < blocks:
        gate_term = gate_term + lax.ppermute(gate_term, "ctx", [(i, i ^ step) for i in range(blocks)])
        step *= 2
    mixed = lax.all_to_all(own_out.reshape(heads, part, 3 * width), "head", 0, 0, tiled=True)
    homes = [lax.ppermute(halo_outs[r], AXES, back(r, blocks, heads)) for r in range(heads)]

    at = jnp.stack([rows * block + part * me]).astype(jnp.int32)
    grad_queries, grad_keys, grad_values = choose(at, span, mixed, homes, heads, width)
    return grad_queries, grad_keys, grad_values, gate_term


def solution(mesh):
    rows, columns = P(AXES, None), P(None, "head")
    return jax.shard_map(
        functools.partial(shards, mesh.shape["head"]),
        mesh=mesh,
        in_specs=(rows, rows, rows, rows, columns, P()),
        out_specs=(rows, rows, rows, columns),
        check_vma=False,
    )
```
